32 devices in a mesh: frames: 8 (over y, x, core), heads: 4 (over z).
Axes of the slice: x: 2, y: 2, z: 4, core: 2. Of those that a mesh axis runs over, the one named last changes fastest.
Arguments:
- frames: bfloat16 [8192, 1152], P('frames', 'heads'), may hold values from -6 to 6
- latents: bfloat16 [256, 1152], P('frames'), may hold values from -400 to 400
- w_query: bfloat16 [1152, 4096], P(None, 'heads'), may hold values from -0.1875 to 0.1875
- w_key: bfloat16 [1152, 4096], P(None, 'heads'), may hold values from -0.1875 to 0.1875
- w_value: bfloat16 [1152, 4096], P(None, 'heads'), may hold values from -0.1875 to 0.1875
- w_out: bfloat16 [4096, 8192], P('heads', 'frames'), may hold values from -0.09375 to 0.09375
- norm_gain: float32 [8192], P('frames'), may hold values from 0.5 to 1.5
- w_gate: bfloat16 [8192, 16384], P('frames', 'heads'), may hold values from -0.0625 to 0.0625
- w_up: bfloat16 [8192, 16384], P('frames', 'heads'), may hold values from -0.0625 to 0.0625
- w_down: bfloat16 [16384, 8192], P('heads', 'frames'), may hold values from -0.046875 to 0.046875
Outputs:
- block_out: bfloat16 [256, 8192], P('heads', 'frames')
The draws below stay inside these ranges and needn't reach their ends.
All inputs are finite; a program needn't handle non-finite values.
Results may differ from the reference program's by a relative error of at most 0.023.
Values may be sent and summed in bfloat16 or wider, within the bound.
A program may use at most 128 MiB of HBM per device.

```python
import jax
import jax.numpy as jnp
from jax import lax

VIS = 1152
NHEAD = 32
HDIM = 128
D = 8192
FF = 16384
LAT = 256
TOKENS = 8192
INNER = 4096


def draw_latents(key, part):
    base = jnp.clip(jax.random.normal(key, (LAT, VIS), jnp.float32), -6.0, 6.0)
    return base.astype(jnp.bfloat16)


def levels(rng, shape, cuts, smallest, top_value):
    def one(axis_at, parts):
        heights = jax.random.uniform(jax.random.fold_in(jax.random.fold_in(rng, 6), axis_at), (parts,), jnp.float32, smallest / len(cuts), top_value / len(cuts))
        return jnp.repeat(jnp.exp(heights), shape[axis_at] // parts).reshape((-1,) + (1,) * (len(shape) - axis_at - 1))

    gain = one(*cuts[0])
    for cut in cuts[1:]:
        gain = gain * one(*cut)
    return gain


def scatter_about(stream_key, shape, scale, bound, split=(), dtype=jnp.bfloat16):
    result = jax.random.normal(stream_key, shape, jnp.float32) * scale
    if len(split) > 0:
        result = levels(stream_key, shape, split, -0.22, 0.18) * result
    return jnp.clip(result, min=-bound, max=bound).astype(dtype)


def setup_inputs(seed: int = 0) -> dict:
    arg_keys = jax.random.split(jax.random.key(seed), 11)
    frames = scatter_about(arg_keys[0], (TOKENS, VIS), 1.0, 6.0, ((0, 8), (1, 4)))
    latents = draw_latents(jax.random.fold_in(arg_keys[10], 71), 0)
    w_query = scatter_about(arg_keys[2], (VIS, INNER), VIS ** -0.5, 0.1875, ((1, 4),))
    w_key = scatter_about(arg_keys[3], (VIS, INNER), VIS ** -0.5, 0.1875, ((1, 4),))
    w_value = scatter_about(arg_keys[4], (VIS, INNER), VIS ** -0.5, 0.1875, ((1, 4),))
    w_out = scatter_about(arg_keys[5], (INNER, D), INNER ** -0.5, 0.09375, ((0, 4), (1, 8)))
    norm_gain = jnp.clip(1.0 + 0.1 * jax.random.normal(arg_keys[6], (D,), jnp.float32), 0.5, 1.5)
    w_gate = scatter_about(arg_keys[7], (D, FF), D ** -0.5, 0.0625, ((0, 8), (1, 4)))
    w_up = scatter_about(arg_keys[8], (D, FF), D ** -0.5, 0.0625, ((0, 8), (1, 4)))
    w_down = scatter_about(arg_keys[9], (FF, D), FF ** -0.5, 0.046875, ((0, 4), (1, 8)))
    return dict(frames=frames, latents=latents, w_query=w_query, w_key=w_key, w_value=w_value, w_out=w_out, norm_gain=norm_gain, w_gate=w_gate, w_up=w_up, w_down=w_down)


norm_eps = 1e-06

def reference(frames, latents, w_query, w_key, w_value, w_out, norm_gain, w_gate, w_up, w_down):
    queries = jnp.dot(latents, w_query, preferred_element_type=jnp.float32).astype(jnp.bfloat16)
    query_heads = queries.reshape(LAT, NHEAD, HDIM).transpose(1, 0, 2)
    key_weights = w_key.reshape(VIS, NHEAD, HDIM).transpose(1, 0, 2)
    value_weights = w_value.reshape(VIS, NHEAD, HDIM).transpose(1, 0, 2)

    def attend(inputs):
        query_head, key_weight, value_weight = inputs
        keys = jnp.dot(frames, key_weight, preferred_element_type=jnp.float32).astype(jnp.bfloat16)
        values = jnp.dot(frames, value_weight, preferred_element_type=jnp.float32).astype(jnp.bfloat16)
        scores = jnp.dot(query_head, keys.T, preferred_element_type=jnp.float32) * HDIM ** (-0.5)
        peak = lax.optimization_barrier(jnp.max(scores, axis=1, keepdims=True))
        weights = jnp.exp(scores - peak)
        total = lax.optimization_barrier(jnp.sum(weights, axis=1, keepdims=True))
        mixed = jnp.dot(weights.astype(jnp.bfloat16), values, preferred_element_type=jnp.float32)
        return (mixed / total).astype(jnp.bfloat16)
    heads_out = lax.map(attend, (query_heads, key_weights, value_weights))
    attention = heads_out.transpose(1, 0, 2).reshape(LAT, INNER)
    latent_state = jnp.dot(attention, w_out, preferred_element_type=jnp.float32).astype(jnp.bfloat16)
    state_float = latent_state.astype(jnp.float32)
    scale_rows = lax.rsqrt(lax.optimization_barrier(jnp.mean(state_float * state_float, axis=1, keepdims=True)) + norm_eps)
    normed = (state_float * norm_gain[None, :]).astype(jnp.bfloat16)
    gate = jnp.dot(normed, w_gate, preferred_element_type=jnp.float32) * scale_rows
    up_part = jnp.dot(normed, w_up, preferred_element_type=jnp.float32) * scale_rows
    hidden = (jax.nn.silu(gate) * up_part).astype(jnp.bfloat16)
    down = jnp.dot(hidden, w_down, preferred_element_type=jnp.float32)
    return (state_float + down).astype(jnp.bfloat16)
```

```python
import math

import jax
import jax.numpy as jnp
from jax import lax
from jax.experimental import pallas as pl
from jax.experimental.pallas import tpu as pltpu
from jax.sharding import PartitionSpec as P

HDIM = 128
norm_eps = 1e-06
F32 = jnp.float32
BF16 = jnp.bfloat16
MIB = 2**20


def rcopy(src, dst, ssem, rsem, axis, peer):
    return pltpu.make_async_remote_copy(
        src_ref=src,
        dst_ref=dst,
        send_sem=ssem,
        recv_sem=rsem,
        device_id={axis: peer},
        device_id_type=pl.DeviceIdType.MESH,
    )


def loop(lo, hi, body):
    def step(i, carry):
        body(i)
        return carry

    lax.fori_loop(lo, hi, step, 0)


def flat(value):
    rows, cols = value.shape[-2], value.shape[-1]
    if rows % 16:
        return value.astype(F32).reshape(-1, cols).astype(value.dtype)
    return value.reshape(-1, cols)


def tile_of(size, want):
    return want if size % want == 0 else size


def attend_kernel(
    nf, nh,
    fr, lat, wq, wk, wv,
    mix_out, stat_out,
    fr_all, q_all, wq_v, wkv, acc,
    w_sem, rs_sem, ls_sem, fr_sem, qs_sem, qr_sem,
):
    me = lax.axis_index("frames")
    hz = lax.axis_index("heads")
    width = wq.shape[1]
    heads = width // HDIM
    tokens = fr.shape[0]

    c_q = pltpu.make_async_copy(wq, wq_v, w_sem.at[0])
    c_k = pltpu.make_async_copy(wk, wkv.at[0], w_sem.at[1])
    c_v = pltpu.make_async_copy(wv, wkv.at[1], w_sem.at[2])
    c_q.start()
    c_k.start()
    c_v.start()

    barrier = pltpu.get_barrier_semaphore()

    def greet(d):
        pl.semaphore_signal(
            barrier, inc=1, device_id={"frames": lax.rem(me + d, nf)},
            device_id_type=pl.DeviceIdType.MESH)

    loop(1, nf, greet)
    has_l = hz > 0
    has_r = hz < nh - 1

    @pl.when(has_l)
    def _():
        pl.semaphore_signal(barrier, inc=1, device_id={"heads": hz - 1},
                            device_id_type=pl.DeviceIdType.MESH)

    @pl.when(has_r)
    def _():
        pl.semaphore_signal(barrier, inc=1, device_id={"heads": hz + 1},
                            device_id_type=pl.DeviceIdType.MESH)

    pl.semaphore_wait(barrier, nf - 1 + has_l.astype(jnp.int32) + has_r.astype(jnp.int32))

    def right(s, src, b):
        return rcopy(src, fr_all.at[b], rs_sem.at[s], fr_sem.at[b], "heads", hz + 1)

    def left(s, src, b):
        return rcopy(src, fr_all.at[b], ls_sem.at[s], fr_sem.at[b], "heads", hz - 1)

    @pl.when(has_r)
    def _():
        right(0, fr, hz).start()

    @pl.when(has_l)
    def _():
        left(0, fr, hz).start()

    c_q.wait()
    q_all[me] = jnp.dot(lat[...], wq_v[...], preferred_element_type=F32).astype(BF16)

    def qcopy(d):
        return rcopy(q_all.at[me], q_all.at[me], qs_sem.at[d], qr_sem.at[d],
                     "frames", lax.rem(me + d, nf))

    loop(1, nf, lambda d: qcopy(d).start())
    c_k.wait()
    c_v.wait()

    tt = tile_of(tokens, 256)

    def project(x, b, first):
        def tile(i):
            rows = pl.ds(pl.multiple_of(i * tt, tt), tt)
            xb = x[rows, :]
            for w in range(2):
                term = jnp.dot(xb, wkv[w, b], preferred_element_type=F32)
                if first:
                    acc[w, rows, :] = term
                else:
                    acc[w, rows, :] += term
        loop(0, tokens // tt, tile)

    project(fr, hz, True)

    def hop(s):
        lb, rb = hz - s, hz + s

        @pl.when(lb >= 0)
        def _():
            right(s, fr, lb).wait_recv()

            @pl.when(has_r)
            def _():
                right(s, fr_all.at[lb], lb).start()

        @pl.when(rb < nh)
        def _():
            right(s, fr, rb).wait_recv()

            @pl.when(has_l)
            def _():
                left(s, fr_all.at[rb], rb).start()

        @pl.when(lb >= 0)
        def _():
            project(fr_all.at[lb], lb, False)

        @pl.when(rb < nh)
        def _():
            project(fr_all.at[rb], rb, False)

    loop(1, nh, hop)
    loop(1, nf, lambda d: qcopy(d).wait_recv())

    scale = HDIM ** (-0.5)
    latents = mix_out.shape[0]
    lane = lax.broadcasted_iota(jnp.int32, (latents, 128), 1)
    peaks = jnp.zeros((latents, 128), F32)
    sums = jnp.ones((latents, 128), F32)
    for h in range(heads):
        cols = slice(h * HDIM, (h + 1) * HDIM)
        q = flat(q_all[:, :, cols])
        k = acc[0, :, cols].astype(BF16)
        v = acc[1, :, cols].astype(BF16)
        scores = lax.dot_general(q, k, (((1,), (1,)), ((), ())),
                                 preferred_element_type=F32) * scale
        peak = jnp.max(scores, axis=1, keepdims=True)
        weights = jnp.exp(scores - peak)
        total = jnp.sum(weights, axis=1, keepdims=True)
        mixed = jnp.dot(weights.astype(BF16), v, preferred_element_type=F32)
        mix_out[:, cols] = (mixed / total).astype(BF16)
        peaks = jnp.where(lane == h, peak, peaks)
        sums = jnp.where(lane == h, total, sums)
    stat_out[:, :128] = peaks
    stat_out[:, 128:] = sums

    loop(1, nf, lambda d: qcopy(d).wait_send())

    def drain(s):
        @pl.when((hz - s >= 0) & has_r)
        def _():
            right(s, fr, hz).wait_send()

        @pl.when((hz + s < nh) & has_l)
        def _():
            left(s, fr, hz).wait_send()

    loop(0, nh, drain)


def block_kernel(
    nf, nh, ny, nx,
    mix, stat, gain, w_out, w_gate, w_up, w_down,
    out,
    wo, wg, wu, wd,
    rm, rst, att_all, part, rz, lat_all, nrm, sqp, rsq,
    gu, rc, r2a, r2b, s2a, s2b, r3a, r3b, hid, dp, rd,
    w_sem, mix_s, mix_r, st_s, st_r, at_s, at_r, z_s, z_r, l_s, l_r, sq_s, sq_r,
    c_s, c_r, x2_s, x2_r, y2_s, y2_r, x3_s, x3_r, y3_s, y3_r,
    hy_s, hy_r, hx_s, hx_r, gx_s, gx_r, gy_s, gy_r, hc_s, hc_r, d_s, d_r,
):
    me = lax.axis_index("frames")
    hz = lax.axis_index("heads")
    core = lax.rem(me, 2)
    xi = lax.rem(me // 2, nx)
    yi = me // (2 * nx)
    r, width = mix.shape[1], mix.shape[2]
    heads = width // HDIM
    fh = nf // nh
    cols_d = wo.shape[1]
    units = wg.shape[1]
    half = units // 2
    latents = nf * r

    copies = [
        pltpu.make_async_copy(src, dst, w_sem.at[i])
        for i, (src, dst) in enumerate(
            [(w_out, wo), (w_gate, wg), (w_up, wu), (w_down, wd)])
    ]
    for c in copies:
        c.start()

    barrier = pltpu.get_barrier_semaphore()

    def fpeer(d):
        return lax.rem(me + d, nf)

    def zpeer(d):
        return lax.rem(hz + d, nh)

    def xpeer(d):
        return lax.rem(xi + d, nx)

    def ypeer(d):
        return lax.rem(yi + d, ny)

    def xdev(x):
        return (yi * nx + x) * 2 + core

    def ydev(y):
        return (y * nx + xi) * 2 + core

    def greet_f(d):
        pl.semaphore_signal(barrier, inc=1, device_id={"frames": fpeer(d)},
                            device_id_type=pl.DeviceIdType.MESH)

    def greet_z(d):
        pl.semaphore_signal(barrier, inc=1, device_id={"heads": zpeer(d)},
                            device_id_type=pl.DeviceIdType.MESH)

    loop(1, nf, greet_f)
    loop(1, nh, greet_z)
    pl.semaphore_wait(barrier, nf + nh - 2)

    def mcopy(d):
        return rcopy(mix.at[fpeer(d)], rm.at[d], mix_s.at[d], mix_r.at[d], "frames", fpeer(d))

    def scopy(d):
        return rcopy(stat.at[fpeer(d)], rst.at[d], st_s.at[d], st_r.at[d], "frames", fpeer(d))

    def send_mix(d):
        scopy(d).start()
        mcopy(d).start()

    loop(1, nf, send_mix)
    rm[0] = mix[me]
    rst[0] = stat[me]
    loop(1, nf, lambda d: scopy(d).wait_recv())
    peak = rst[0, :, :128]
    for d in range(1, nf):
        peak = jnp.maximum(peak, rst[d, :, :128])
    loop(1, nf, lambda d: mcopy(d).wait_recv())
    num = [jnp.zeros((r, HDIM), F32) for _ in range(heads)]
    den = jnp.zeros((r, 128), F32)
    for d in range(nf):
        share = jnp.exp(rst[d, :, :128] - peak) * rst[d, :, 128:]
        den = den + share
        for h in range(heads):
            num[h] = num[h] + share[:, h:h + 1] * rm[d, :, h * HDIM:(h + 1) * HDIM].astype(F32)
    for h in range(heads):
        att_all[me, :, h * HDIM:(h + 1) * HDIM] = (num[h] / den[:, h:h + 1]).astype(BF16)

    def acopy(d):
        return rcopy(att_all.at[me], att_all.at[me], at_s.at[d], at_r.at[d], "frames", fpeer(d))

    loop(1, nf, lambda d: acopy(d).start())
    loop(1, nf, lambda d: acopy(d).wait_recv())

    copies[0].wait()
    att = flat(att_all[...])
    tile = tile_of(cols_d, 512)
    for t in range(cols_d // tile):
        cs = slice(t * tile, (t + 1) * tile)
        res = jnp.dot(att, wo[:, cs], preferred_element_type=F32)
        part[:, :, cs] = res.reshape(nh, latents // nh, tile).astype(BF16)

    def zcopy(d):
        return rcopy(part.at[zpeer(d)], rz.at[d], z_s.at[d], z_r.at[d], "heads", zpeer(d))

    loop(1, nh, lambda d: zcopy(d).start())
    loop(1, nh, lambda d: zcopy(d).wait_recv())
    state = part[hz].astype(F32)
    for d in range(1, nh):
        state = state + rz[d].astype(F32)
    lat_all[hz] = state.astype(BF16)

    def lcopy(d):
        return rcopy(lat_all.at[hz], lat_all.at[hz], l_s.at[d], l_r.at[d], "heads", zpeer(d))

    loop(1, nh, lambda d: lcopy(d).start())
    loop(1, nh, lambda d: lcopy(d).wait_recv())

    full = lat_all[...].astype(F32).reshape(latents, cols_d)
    nrm[...] = (full * gain[...]).astype(BF16)
    squares = jnp.sum(full * full, axis=1, keepdims=True)
    sqp[...] = jnp.broadcast_to(squares, (latents, 128)).reshape(nf, r, 128)

    def qcopy(d):
        return rcopy(sqp.at[fpeer(d)], rsq.at[d], sq_s.at[d], sq_r.at[d], "frames", fpeer(d))

    loop(1, nf, lambda d: qcopy(d).start())

    copies[1].wait()
    copies[2].wait()
    gt = tile_of(half, 512)

    def ccopy(t):
        return rcopy(gu.at[t, 1 - core], rc.at[t], c_s.at[t], c_r.at[t],
                     "frames", me + 1 - 2 * core)

    for t in range(2):
        for j in range(2):
            weight = (wg, wu)[j]

            def step(k, t=t, j=j, weight=weight):
                src = pl.ds(pl.multiple_of(t * half + k * gt, gt), gt)
                dst = pl.ds(pl.multiple_of(j * half + k * gt, gt), gt)
                res = jnp.dot(nrm[...], weight[:, src], preferred_element_type=F32)
                res = res.reshape(ny, nx, 2, r, gt).astype(BF16)
                for c in range(2):
                    gu[t, c, :, :, :, dst] = res[:, :, c]

            loop(0, half // gt, step)
        ccopy(t).start()

    def x2copy(d):
        return rcopy(gu.at[0, core, :, xpeer(d)], r2a.at[d], x2_s.at[d], x2_r.at[d],
                     "frames", xdev(xpeer(d)))

    def y2copy(d):
        return rcopy(gu.at[1, core, ypeer(d)], r2b.at[d], y2_s.at[d], y2_r.at[d],
                     "frames", ydev(ypeer(d)))

    def merge(t):
        ccopy(t).wait_recv()
        for y in range(ny):
            for x in range(nx):
                gu[t, core, y, x] = (
                    gu[t, core, y, x].astype(F32) + rc[t, y, x].astype(F32)).astype(BF16)

    merge(0)
    loop(1, nx, lambda d: x2copy(d).start())
    merge(1)
    loop(1, ny, lambda d: y2copy(d).start())

    def y3copy(d):
        return rcopy(s2a.at[ypeer(d)], r3a.at[d], y3_s.at[d], y3_r.at[d],
                     "frames", ydev(ypeer(d)))

    def x3copy(d):
        return rcopy(s2b.at[xpeer(d)], r3b.at[d], x3_s.at[d], x3_r.at[d],
                     "frames", xdev(xpeer(d)))

    loop(1, nx, lambda d: x2copy(d).wait_recv())
    for y in range(ny):
        total = gu[0, core, y, xi].astype(F32)
        for d in range(1, nx):
            total = total + r2a[d, y].astype(F32)
        s2a[y] = total.astype(BF16)
    loop(1, ny, lambda d: y3copy(d).start())
    loop(1, ny, lambda d: y2copy(d).wait_recv())
    for x in range(nx):
        total = gu[1, core, yi, x].astype(F32)
        for d in range(1, ny):
            total = total + r2b[d, x].astype(F32)
        s2b[x] = total.astype(BF16)
    loop(1, nx, lambda d: x3copy(d).start())

    loop(1, nf, lambda d: qcopy(d).wait_recv())
    ssum = sqp[me]
    for d in range(1, nf):
        ssum = ssum + rsq[d]
    scale = lax.rsqrt(ssum[:, :1] / (cols_d * nf) + norm_eps)

    def activate(t, total):
        gate = total[:, :half] * scale
        up = total[:, half:] * scale
        hid[t, core, yi, xi] = (gate / (1.0 + jnp.exp(-gate)) * up).astype(BF16)

    def hycopy(d):
        block = hid.at[0, core, yi, xi]
        return rcopy(block, block, hy_s.at[d], hy_r.at[d], "frames", ydev(ypeer(d)))

    def hxcopy(d):
        block = hid.at[1, core, yi, xi]
        return rcopy(block, block, hx_s.at[d], hx_r.at[d], "frames", xdev(xpeer(d)))

    def gxcopy(d):
        block = hid.at[0, core, :, xi]
        return rcopy(block, block, gx_s.at[d], gx_r.at[d], "frames", xdev(xpeer(d)))

    def gycopy(d):
        block = hid.at[1, core, yi]
        return rcopy(block, block, gy_s.at[d], gy_r.at[d], "frames", ydev(ypeer(d)))

    def hccopy(t):
        block = hid.at[t, core]
        return rcopy(block, block, hc_s.at[t], hc_r.at[t], "frames", me + 1 - 2 * core)

    loop(1, ny, lambda d: y3copy(d).wait_recv())
    total = s2a[yi].astype(F32)
    for d in range(1, ny):
        total = total + r3a[d].astype(F32)
    activate(0, total)
    loop(1, ny, lambda d: hycopy(d).start())
    loop(1, nx, lambda d: x3copy(d).wait_recv())
    total = s2b[xi].astype(F32)
    for d in range(1, nx):
        total = total + r3b[d].astype(F32)
    activate(1, total)
    loop(1, nx, lambda d: hxcopy(d).start())
    loop(1, ny, lambda d: hycopy(d).wait_recv())
    loop(1, nx, lambda d: gxcopy(d).start())
    loop(1, nx, lambda d: hxcopy(d).wait_recv())
    loop(1, ny, lambda d: gycopy(d).start())
    loop(1, nx, lambda d: gxcopy(d).wait_recv())
    hccopy(0).start()
    loop(1, ny, lambda d: gycopy(d).wait_recv())
    hccopy(1).start()
    copies[3].wait()
    hccopy(0).wait_recv()
    hccopy(1).wait_recv()

    dt = tile_of(cols_d, 256)

    def down(k):
        cs = pl.ds(pl.multiple_of(k * dt, dt), dt)
        res = jnp.dot(flat(hid[0]), wd[:half, cs], preferred_element_type=F32)
        res = res + jnp.dot(flat(hid[1]), wd[half:, cs], preferred_element_type=F32)
        res = res.reshape(2, nf // 2, r, dt).astype(BF16)
        for b in range(nf):
            dp[b, :, cs] = res[b % 2, b // 2]

    loop(0, cols_d // dt, down)

    def dcopy(d):
        return rcopy(dp.at[pl.ds(zpeer(d) * fh, fh)], rd.at[d], d_s.at[d], d_r.at[d],
                     "heads", zpeer(d))

    loop(1, nh, lambda d: dcopy(d).start())
    loop(1, nh, lambda d: dcopy(d).wait_recv())
    total = lat_all[hz].astype(F32).reshape(fh, r, cols_d) + dp[pl.ds(hz * fh, fh)].astype(F32)
    for d in range(1, nh):
        total = total + rd[d].astype(F32)
    out[...] = total.astype(BF16)

    def drain_f(d):
        scopy(d).wait_send()
        mcopy(d).wait_send()
        acopy(d).wait_send()
        qcopy(d).wait_send()

    def drain_z(d):
        zcopy(d).wait_send()
        lcopy(d).wait_send()
        dcopy(d).wait_send()

    def drain_x(d):
        x2copy(d).wait_send()
        x3copy(d).wait_send()
        hxcopy(d).wait_send()
        gxcopy(d).wait_send()

    def drain_y(d):
        y2copy(d).wait_send()
        y3copy(d).wait_send()
        hycopy(d).wait_send()
        gycopy(d).wait_send()

    loop(1, nf, drain_f)
    loop(1, nh, drain_z)
    loop(1, nx, drain_x)
    loop(1, ny, drain_y)
    for t in range(2):
        ccopy(t).wait_send()
        hccopy(t).wait_send()


def solution(mesh):
    nf, nh = mesh.shape["frames"], mesh.shape["heads"]
    chips = nf // 2
    nx = max(k for k in range(1, math.isqrt(chips) + 1) if chips % k == 0)
    ny = chips // nx
    vmem = pl.BlockSpec(memory_space=pltpu.VMEM)
    any_ = pl.BlockSpec(memory_space=pl.ANY)
    dma = pltpu.SemaphoreType.DMA

    def on_device(frames, latents, w_query, w_key, w_value, w_out, norm_gain, w_gate, w_up, w_down):
        tokens, feats = frames.shape
        r = latents.shape[0]
        width = w_key.shape[1]
        rows = r * nf
        mix, stat = pl.pallas_call(
            lambda *refs: attend_kernel(nf, nh, *refs),
            out_shape=[
                jax.ShapeDtypeStruct((rows, width), BF16),
                jax.ShapeDtypeStruct((rows, 256), F32),
            ],
            in_specs=[vmem, vmem, any_, any_, any_],
            out_specs=[vmem, vmem],
            scratch_shapes=[
                pltpu.VMEM((nh, tokens, feats), BF16),
                pltpu.VMEM((nf, r, width), BF16),
                pltpu.VMEM(w_query.shape, BF16),
                pltpu.VMEM((2, nh, feats, width), BF16),
                pltpu.VMEM((2, tokens, width), F32),
                dma((3,)), dma((nh,)), dma((nh,)), dma((nh,)), dma((nf,)), dma((nf,)),
            ],
            compiler_params=pltpu.CompilerParams(
                collective_id=0, has_side_effects=True, vmem_limit_bytes=48 * MIB),
            name="attend",
        )(
            frames, latents, w_query,
            w_key.reshape(nh, feats, width), w_value.reshape(nh, feats, width),
        )
        cols_d = w_out.shape[1]
        units = w_gate.shape[1]
        half = units // 2
        fh = nf // nh
        out = pl.pallas_call(
            lambda *refs: block_kernel(nf, nh, ny, nx, *refs),
            out_shape=jax.ShapeDtypeStruct((fh, r, cols_d), BF16),
            in_specs=[vmem, vmem, vmem, any_, any_, any_, any_],
            out_specs=vmem,
            scratch_shapes=[
                pltpu.VMEM(w_out.shape, BF16),
                pltpu.VMEM(w_gate.shape, BF16),
                pltpu.VMEM(w_up.shape, BF16),
                pltpu.VMEM(w_down.shape, BF16),
                pltpu.VMEM((nf, r, width), BF16),
                pltpu.VMEM((nf, r, 256), F32),
                pltpu.VMEM((nf, r, width), BF16),
                pltpu.VMEM((nh, rows // nh, cols_d), BF16),
                pltpu.VMEM((nh, rows // nh, cols_d), BF16),
                pltpu.VMEM((nh, rows // nh, cols_d), BF16),
                pltpu.VMEM((rows, cols_d), BF16),
                pltpu.VMEM((nf, r, 128), F32),
                pltpu.VMEM((nf, r, 128), F32),
                pltpu.VMEM((2, 2, ny, nx, r, units), BF16),
                pltpu.VMEM((2, ny, nx, r, units), BF16),
                pltpu.VMEM((nx, ny, r, units), BF16),
                pltpu.VMEM((ny, nx, r, units), BF16),
                pltpu.VMEM((ny, r, units), BF16),
                pltpu.VMEM((nx, r, units), BF16),
                pltpu.VMEM((ny, r, units), BF16),
                pltpu.VMEM((nx, r, units), BF16),
                pltpu.VMEM((2, 2, ny, nx, r, half), BF16),
                pltpu.VMEM((nf, r, cols_d), BF16),
                pltpu.VMEM((nh, fh, r, cols_d), BF16),
                dma((4,)),
                *[dma((n,)) for n in (
                    nf, nf, nf, nf, nf, nf, nh, nh, nh, nh, nf, nf,
                    2, 2, nx, nx, ny, ny, nx, nx, ny, ny,
                    ny, ny, nx, nx, nx, nx, ny, ny, 2, 2, nh, nh)],
            ],
            compiler_params=pltpu.CompilerParams(
                collective_id=1, has_side_effects=True, vmem_limit_bytes=58 * MIB),
            name="block",
        )(
            mix.reshape(nf, r, width), stat.reshape(nf, r, 256),
            norm_gain.reshape(1, -1), w_out, w_gate, w_up, w_down,
        )
        return out.reshape(rows // nh, cols_d)

    placed = (
        P("frames", "heads"), P("frames", None), P(None, "heads"), P(None, "heads"),
        P(None, "heads"), P("heads", "frames"), P("frames"), P("frames", "heads"),
        P("frames", "heads"), P("heads", "frames"),
    )
    return jax.shard_map(
        on_device, mesh=mesh, in_specs=placed, out_specs=P("heads", "frames"), check_vma=False
    )
```

```python
import math

import jax
import jax.numpy as jnp
from jax import lax
from jax.experimental import pallas as pl
from jax.experimental.pallas import tpu as pltpu
from jax.sharding import PartitionSpec as P

HDIM = 128
norm_eps = 1e-06
F32 = jnp.float32
BF16 = jnp.bfloat16
MIB = 2**20


def rcopy(src, dst, ssem, rsem, axis, peer):
    return pltpu.make_async_remote_copy(
        src_ref=src,
        dst_ref=dst,
        send_sem=ssem,
        recv_sem=rsem,
        device_id={axis: peer},
        device_id_type=pl.DeviceIdType.MESH,
    )


def loop(lo, hi, body):
    def step(i, carry):
        body(i)
        return carry

    lax.fori_loop(lo, hi, step, 0)


def flat(value):
    rows, cols = value.shape[-2], value.shape[-1]
    if rows % 16:
        return value.astype(F32).reshape(-1, cols).astype(value.dtype)
    return value.reshape(-1, cols)


def tile_of(size, want):
    return want if size % want == 0 else size


def attend_kernel(
    nf, nh, ng,
    fr, lat, wq, wk, wv,
    mix_out, stat_out,
    fr_all, q_all, wq_v, wkv, acc,
    w_sem, rs_sem, ls_sem, fr_sem, qs_sem, qr_sem,
):
    me = lax.axis_index("frames")
    hz = lax.axis_index("heads")
    width = wq.shape[1]
    heads = width // HDIM
    tokens = fr.shape[0]

    c_q = pltpu.make_async_copy(wq, wq_v, w_sem.at[0])
    c_k = pltpu.make_async_copy(wk, wkv.at[0], w_sem.at[1])
    c_v = pltpu.make_async_copy(wv, wkv.at[1], w_sem.at[2])
    c_q.start()
    c_k.start()
    c_v.start()

    barrier = pltpu.get_barrier_semaphore()

    def greet(d):
        pl.semaphore_signal(
            barrier, inc=1, device_id={"frames": lax.rem(me + d, nf)},
            device_id_type=pl.DeviceIdType.MESH)

    loop(1, nf, greet)
    has_l = hz > 0
    has_r = hz < nh - 1

    @pl.when(has_l)
    def _():
        pl.semaphore_signal(barrier, inc=1, device_id={"heads": hz - 1},
                            device_id_type=pl.DeviceIdType.MESH)

    @pl.when(has_r)
    def _():
        pl.semaphore_signal(barrier, inc=1, device_id={"heads": hz + 1},
                            device_id_type=pl.DeviceIdType.MESH)

    pl.semaphore_wait(barrier, nf - 1 + has_l.astype(jnp.int32) + has_r.astype(jnp.int32))

    def right(s, src, b):
        return rcopy(src, fr_all.at[b], rs_sem.at[s], fr_sem.at[b], "heads", hz + 1)

    def left(s, src, b):
        return rcopy(src, fr_all.at[b], ls_sem.at[s], fr_sem.at[b], "heads", hz - 1)

    @pl.when(has_r)
    def _():
        right(0, fr, hz).start()

    @pl.when(has_l)
    def _():
        left(0, fr, hz).start()

    c_q.wait()
    fh = nf // nh
    per = fh // ng
    inner = lax.rem(me, fh)
    slot = (inner // per * nh + me // fh) * per + lax.rem(inner, per)
    q_all[slot] = jnp.dot(lat[...], wq_v[...], preferred_element_type=F32).astype(BF16)

    def qcopy(d):
        return rcopy(q_all.at[slot], q_all.at[slot], qs_sem.at[d], qr_sem.at[d],
                     "frames", lax.rem(me + d, nf))

    loop(1, nf, lambda d: qcopy(d).start())
    c_k.wait()
    c_v.wait()

    tt = tile_of(tokens, 256)

    def project(x, b, first):
        def tile(i):
            rows = pl.ds(pl.multiple_of(i * tt, tt), tt)
            xb = x[rows, :]
            for w in range(2):
                term = jnp.dot(xb, wkv[w, b], preferred_element_type=F32)
                if first:
                    acc[w, rows, :] = term
                else:
                    acc[w, rows, :] += term
        loop(0, tokens // tt, tile)

    project(fr, hz, True)

    def hop(s):
        lb, rb = hz - s, hz + s

        @pl.when(lb >= 0)
        def _():
            right(s, fr, lb).wait_recv()

            @pl.when(has_r)
            def _():
                right(s, fr_all.at[lb], lb).start()

        @pl.when(rb < nh)
        def _():
            right(s, fr, rb).wait_recv()

            @pl.when(has_l)
            def _():
                left(s, fr_all.at[rb], rb).start()

        @pl.when(lb >= 0)
        def _():
            project(fr_all.at[lb], lb, False)

        @pl.when(rb < nh)
        def _():
            project(fr_all.at[rb], rb, False)

    loop(1, nh, hop)
    loop(1, nf, lambda d: qcopy(d).wait_recv())

    scale = HDIM ** (-0.5)
    latents = mix_out.shape[0]
    lane = lax.broadcasted_iota(jnp.int32, (latents, 128), 1)
    peaks = jnp.zeros((latents, 128), F32)
    sums = jnp.ones((latents, 128), F32)
    for h in range(heads):
        cols = slice(h * HDIM, (h + 1) * HDIM)
        q = flat(q_all[:, :, cols])
        k = acc[0, :, cols].astype(BF16)
        v = acc[1, :, cols].astype(BF16)
        scores = lax.dot_general(q, k, (((1,), (1,)), ((), ())),
                                 preferred_element_type=F32) * scale
        peak = jnp.max(scores, axis=1, keepdims=True)
        weights = jnp.exp(scores - peak)
        total = jnp.sum(weights, axis=1, keepdims=True)
        mixed = jnp.dot(weights.astype(BF16), v, preferred_element_type=F32)
        mix_out[:, cols] = (mixed / total).astype(BF16)
        peaks = jnp.where(lane == h, peak, peaks)
        sums = jnp.where(lane == h, total, sums)
    stat_out[:, :128] = peaks
    stat_out[:, 128:] = sums

    loop(1, nf, lambda d: qcopy(d).wait_send())

    def drain(s):
        @pl.when((hz - s >= 0) & has_r)
        def _():
            right(s, fr, hz).wait_send()

        @pl.when((hz + s < nh) & has_l)
        def _():
            left(s, fr, hz).wait_send()

    loop(0, nh, drain)


def block_kernel(
    nf, nh, ng, ny, nx,
    mix, stat, gain, w_out, w_gate, w_up, w_down,
    out,
    wo, wg, wu, wd,
    rm, rst, att_all, part, rz, lat_all, nrm, sqp, rsq,
    gu, rc, r2a, r2b, s2a, s2b, r3a, r3b, hid, dp, rd,
    w_sem, mix_s, mix_r, st_s, st_r, at_s, at_r, z_s, z_r, l_s, l_r, sq_s, sq_r,
    c_s, c_r, x2_s, x2_r, y2_s, y2_r, x3_s, x3_r, y3_s, y3_r,
    hy_s, hy_r, hx_s, hx_r, gx_s, gx_r, gy_s, gy_r, hc_s, hc_r, d_s, d_r,
):
    me = lax.axis_index("frames")
    hz = lax.axis_index("heads")
    core = lax.rem(me, 2)
    xi = lax.rem(me // 2, nx)
    yi = me // (2 * nx)
    r, width = mix.shape[2], mix.shape[3]
    heads = width // HDIM
    fh = nf // nh
    cols_d = wo.shape[1]
    units = wg.shape[1]
    half = units // 2
    latents = nf * r

    copies = [
        pltpu.make_async_copy(src, dst, w_sem.at[i])
        for i, (src, dst) in enumerate(
            [(w_out, wo), (w_gate, wg), (w_up, wu), (w_down, wd)])
    ]
    for c in copies:
        c.start()

    barrier = pltpu.get_barrier_semaphore()

    def fpeer(d):
        return lax.rem(me + d, nf)

    def zpeer(d):
        return lax.rem(hz + d, nh)

    def xpeer(d):
        return lax.rem(xi + d, nx)

    def ypeer(d):
        return lax.rem(yi + d, ny)

    def xdev(x):
        return (yi * nx + x) * 2 + core

    def ydev(y):
        return (y * nx + xi) * 2 + core

    def greet_f(d):
        pl.semaphore_signal(barrier, inc=1, device_id={"frames": fpeer(d)},
                            device_id_type=pl.DeviceIdType.MESH)

    def greet_z(d):
        pl.semaphore_signal(barrier, inc=1, device_id={"heads": zpeer(d)},
                            device_id_type=pl.DeviceIdType.MESH)

    loop(1, nf, greet_f)
    loop(1, nh, greet_z)
    pl.semaphore_wait(barrier, nf + nh - 2)

    def phases(
        g,
        mix, stat, out, rm, rst, att_all, part, rz, lat_all, nrm, sqp, rsq, gu, rc, r2a, r2b,
        s2a, s2b, r3a, r3b, hid, dp, rd, mix_s, mix_r, st_s, st_r, at_s, at_r, z_s, z_r, l_s,
        l_r, sq_s, sq_r, c_s, c_r, x2_s, x2_r, y2_s, y2_r, x3_s, x3_r, y3_s, y3_r, hy_s, hy_r,
        hx_s, hx_r, gx_s, gx_r, gy_s, gy_r, hc_s, hc_r, d_s, d_r,
    ):
        def mcopy(d):
            return rcopy(mix.at[fpeer(d)], rm.at[d], mix_s.at[d], mix_r.at[d], "frames", fpeer(d))

        def scopy(d):
            return rcopy(stat.at[fpeer(d)], rst.at[d], st_s.at[d], st_r.at[d], "frames", fpeer(d))

        def send_mix(d):
            scopy(d).start()
            mcopy(d).start()

        loop(1, nf, send_mix)
        rm[0] = mix[me]
        rst[0] = stat[me]
        yield
        loop(1, nf, lambda d: scopy(d).wait_recv())
        peak = rst[0, :, :128]
        for d in range(1, nf):
            peak = jnp.maximum(peak, rst[d, :, :128])
        loop(1, nf, lambda d: mcopy(d).wait_recv())
        num = [jnp.zeros((r, HDIM), F32) for _ in range(heads)]
        den = jnp.zeros((r, 128), F32)
        for d in range(nf):
            share = jnp.exp(rst[d, :, :128] - peak) * rst[d, :, 128:]
            den = den + share
            for h in range(heads):
                num[h] = num[h] + share[:, h:h + 1] * rm[d, :, h * HDIM:(h + 1) * HDIM].astype(F32)
        for h in range(heads):
            att_all[me, :, h * HDIM:(h + 1) * HDIM] = (num[h] / den[:, h:h + 1]).astype(BF16)

        def acopy(d):
            return rcopy(att_all.at[me], att_all.at[me], at_s.at[d], at_r.at[d], "frames", fpeer(d))

        loop(1, nf, lambda d: acopy(d).start())
        yield
        loop(1, nf, lambda d: acopy(d).wait_recv())

        if g == 0:
            copies[0].wait()
        att = flat(att_all[...])
        tile = tile_of(cols_d, 512)
        for t in range(cols_d // tile):
            cs = slice(t * tile, (t + 1) * tile)
            res = jnp.dot(att, wo[:, cs], preferred_element_type=F32)
            part[:, :, cs] = res.reshape(nh, latents // nh, tile).astype(BF16)

        def zcopy(d):
            return rcopy(part.at[zpeer(d)], rz.at[d], z_s.at[d], z_r.at[d], "heads", zpeer(d))

        loop(1, nh, lambda d: zcopy(d).start())
        yield
        loop(1, nh, lambda d: zcopy(d).wait_recv())
        state = part[hz].astype(F32)
        for d in range(1, nh):
            state = state + rz[d].astype(F32)
        lat_all[hz] = state.astype(BF16)

        def lcopy(d):
            return rcopy(lat_all.at[hz], lat_all.at[hz], l_s.at[d], l_r.at[d], "heads", zpeer(d))

        loop(1, nh, lambda d: lcopy(d).start())
        yield
        loop(1, nh, lambda d: lcopy(d).wait_recv())

        full = lat_all[...].astype(F32).reshape(latents, cols_d)
        nrm[...] = (full * gain[...]).astype(BF16)
        squares = jnp.sum(full * full, axis=1, keepdims=True)
        sqp[...] = jnp.broadcast_to(squares, (latents, 128)).reshape(nf, r, 128)

        def qcopy(d):
            return rcopy(sqp.at[fpeer(d)], rsq.at[d], sq_s.at[d], sq_r.at[d], "frames", fpeer(d))

        loop(1, nf, lambda d: qcopy(d).start())

        if g == 0:
            copies[1].wait()
            copies[2].wait()
        gt = tile_of(half, 512)

        def ccopy(t):
            return rcopy(gu.at[t, 1 - core], rc.at[t], c_s.at[t], c_r.at[t],
                         "frames", me + 1 - 2 * core)

        for t in range(2):
            for j in range(2):
                weight = (wg, wu)[j]

                def step(k, t=t, j=j, weight=weight):
                    src = pl.ds(pl.multiple_of(t * half + k * gt, gt), gt)
                    dst = pl.ds(pl.multiple_of(j * half + k * gt, gt), gt)
                    res = jnp.dot(nrm[...], weight[:, src], preferred_element_type=F32)
                    res = res.reshape(ny, nx, 2, r, gt).astype(BF16)
                    for c in range(2):
                        gu[t, c, :, :, :, dst] = res[:, :, c]

                loop(0, half // gt, step)
            ccopy(t).start()
        yield

        def x2copy(d):
            return rcopy(gu.at[0, core, :, xpeer(d)], r2a.at[d], x2_s.at[d], x2_r.at[d],
                         "frames", xdev(xpeer(d)))

        def y2copy(d):
            return rcopy(gu.at[1, core, ypeer(d)], r2b.at[d], y2_s.at[d], y2_r.at[d],
                         "frames", ydev(ypeer(d)))

        def merge(t):
            ccopy(t).wait_recv()
            for y in range(ny):
                for x in range(nx):
                    gu[t, core, y, x] = (
                        gu[t, core, y, x].astype(F32) + rc[t, y, x].astype(F32)).astype(BF16)

        merge(0)
        loop(1, nx, lambda d: x2copy(d).start())
        merge(1)
        loop(1, ny, lambda d: y2copy(d).start())
        yield

        def y3copy(d):
            return rcopy(s2a.at[ypeer(d)], r3a.at[d], y3_s.at[d], y3_r.at[d],
                         "frames", ydev(ypeer(d)))

        def x3copy(d):
            return rcopy(s2b.at[xpeer(d)], r3b.at[d], x3_s.at[d], x3_r.at[d],
                         "frames", xdev(xpeer(d)))

        loop(1, nx, lambda d: x2copy(d).wait_recv())
        for y in range(ny):
            total = gu[0, core, y, xi].astype(F32)
            for d in range(1, nx):
                total = total + r2a[d, y].astype(F32)
            s2a[y] = total.astype(BF16)
        loop(1, ny, lambda d: y3copy(d).start())
        loop(1, ny, lambda d: y2copy(d).wait_recv())
        for x in range(nx):
            total = gu[1, core, yi, x].astype(F32)
            for d in range(1, ny):
                total = total + r2b[d, x].astype(F32)
            s2b[x] = total.astype(BF16)
        loop(1, nx, lambda d: x3copy(d).start())
        yield

        loop(1, nf, lambda d: qcopy(d).wait_recv())
        ssum = sqp[me]
        for d in range(1, nf):
            ssum = ssum + rsq[d]
        scale = lax.rsqrt(ssum[:, :1] / (cols_d * nf) + norm_eps)

        def activate(t, total):
            gate = total[:, :half] * scale
            up = total[:, half:] * scale
            hid[t, core, yi, xi] = (gate / (1.0 + jnp.exp(-gate)) * up).astype(BF16)

        def hycopy(d):
            block = hid.at[0, core, yi, xi]
            return rcopy(block, block, hy_s.at[d], hy_r.at[d], "frames", ydev(ypeer(d)))

        def hxcopy(d):
            block = hid.at[1, core, yi, xi]
            return rcopy(block, block, hx_s.at[d], hx_r.at[d], "frames", xdev(xpeer(d)))

        def gxcopy(d):
            block = hid.at[0, core, :, xi]
            return rcopy(block, block, gx_s.at[d], gx_r.at[d], "frames", xdev(xpeer(d)))

        def gycopy(d):
            block = hid.at[1, core, yi]
            return rcopy(block, block, gy_s.at[d], gy_r.at[d], "frames", ydev(ypeer(d)))

        def hccopy(t):
            block = hid.at[t, core]
            return rcopy(block, block, hc_s.at[t], hc_r.at[t], "frames", me + 1 - 2 * core)

        loop(1, ny, lambda d: y3copy(d).wait_recv())
        total = s2a[yi].astype(F32)
        for d in range(1, ny):
            total = total + r3a[d].astype(F32)
        activate(0, total)
        loop(1, ny, lambda d: hycopy(d).start())
        loop(1, nx, lambda d: x3copy(d).wait_recv())
        total = s2b[xi].astype(F32)
        for d in range(1, nx):
            total = total + r3b[d].astype(F32)
        activate(1, total)
        loop(1, nx, lambda d: hxcopy(d).start())
        yield
        loop(1, ny, lambda d: hycopy(d).wait_recv())
        loop(1, nx, lambda d: gxcopy(d).start())
        loop(1, nx, lambda d: hxcopy(d).wait_recv())
        loop(1, ny, lambda d: gycopy(d).start())
        yield
        loop(1, nx, lambda d: gxcopy(d).wait_recv())
        hccopy(0).start()
        loop(1, ny, lambda d: gycopy(d).wait_recv())
        hccopy(1).start()
        yield
        if g == 0:
            copies[3].wait()
        hccopy(0).wait_recv()
        hccopy(1).wait_recv()

        dt = tile_of(cols_d, 256)

        def down(k):
            cs = pl.ds(pl.multiple_of(k * dt, dt), dt)
            res = jnp.dot(flat(hid[0]), wd[:half, cs], preferred_element_type=F32)
            res = res + jnp.dot(flat(hid[1]), wd[half:, cs], preferred_element_type=F32)
            res = res.reshape(2, nf // 2, r, dt).astype(BF16)
            for b in range(nf):
                dp[b, :, cs] = res[b % 2, b // 2]

        loop(0, cols_d // dt, down)

        def dcopy(d):
            return rcopy(dp.at[pl.ds(zpeer(d) * fh, fh)], rd.at[d], d_s.at[d], d_r.at[d],
                         "heads", zpeer(d))

        loop(1, nh, lambda d: dcopy(d).start())
        yield
        loop(1, nh, lambda d: dcopy(d).wait_recv())
        total = lat_all[hz].astype(F32).reshape(fh, r, cols_d) + dp[pl.ds(hz * fh, fh)].astype(F32)
        for d in range(1, nh):
            total = total + rd[d].astype(F32)
        out[...] = total.astype(BF16)

        def drain_f(d):
            scopy(d).wait_send()
            mcopy(d).wait_send()
            acopy(d).wait_send()
            qcopy(d).wait_send()

        def drain_z(d):
            zcopy(d).wait_send()
            lcopy(d).wait_send()
            dcopy(d).wait_send()

        def drain_x(d):
            x2copy(d).wait_send()
            x3copy(d).wait_send()
            hxcopy(d).wait_send()
            gxcopy(d).wait_send()

        def drain_y(d):
            y2copy(d).wait_send()
            y3copy(d).wait_send()
            hycopy(d).wait_send()
            gycopy(d).wait_send()

        loop(1, nf, drain_f)
        loop(1, nh, drain_z)
        loop(1, nx, drain_x)
        loop(1, ny, drain_y)
        for t in range(2):
            ccopy(t).wait_send()
            hccopy(t).wait_send()

    views = [
        mix, stat, out, rm, rst, att_all, part, rz, lat_all, nrm, sqp, rsq, gu, rc, r2a, r2b,
        s2a, s2b, r3a, r3b, hid, dp, rd, mix_s, mix_r, st_s, st_r, at_s, at_r, z_s, z_r, l_s,
        l_r, sq_s, sq_r, c_s, c_r, x2_s, x2_r, y2_s, y2_r, x3_s, x3_r, y3_s, y3_r, hy_s, hy_r,
        hx_s, hx_r, gx_s, gx_r, gy_s, gy_r, hc_s, hc_r, d_s, d_r,
    ]
    running = [phases(g, *[v.at[g] for v in views]) for g in range(ng)]
    while running:
        running = [p for p in running if next(p, running) is None]


def solution(mesh):
    nf, nh = mesh.shape["frames"], mesh.shape["heads"]
    chips = nf // 2
    nx = max(k for k in range(1, math.isqrt(chips) + 1) if chips % k == 0)
    ny = chips // nx
    vmem = pl.BlockSpec(memory_space=pltpu.VMEM)
    any_ = pl.BlockSpec(memory_space=pl.ANY)
    dma = pltpu.SemaphoreType.DMA

    def on_device(frames, latents, w_query, w_key, w_value, w_out, norm_gain, w_gate, w_up, w_down):
        tokens, feats = frames.shape
        r = latents.shape[0]
        width = w_key.shape[1]
        rows = r * nf
        ng = 2 if (nf // nh) % 2 == 0 and r % 32 == 0 else 1
        rg = r // ng
        mix, stat = pl.pallas_call(
            lambda *refs: attend_kernel(nf, nh, ng, *refs),
            out_shape=[
                jax.ShapeDtypeStruct((rows, width), BF16),
                jax.ShapeDtypeStruct((rows, 256), F32),
            ],
            in_specs=[vmem, vmem, any_, any_, any_],
            out_specs=[vmem, vmem],
            scratch_shapes=[
                pltpu.VMEM((nh, tokens, feats), BF16),
                pltpu.VMEM((nf, r, width), BF16),
                pltpu.VMEM(w_query.shape, BF16),
                pltpu.VMEM((2, nh, feats, width), BF16),
                pltpu.VMEM((2, tokens, width), F32),
                dma((3,)), dma((nh,)), dma((nh,)), dma((nh,)), dma((nf,)), dma((nf,)),
            ],
            compiler_params=pltpu.CompilerParams(
                collective_id=0, has_side_effects=True, vmem_limit_bytes=48 * MIB),
            name="attend",
        )(
            frames, latents, w_query,
            w_key.reshape(nh, feats, width), w_value.reshape(nh, feats, width),
        )
        cols_d = w_out.shape[1]
        units = w_gate.shape[1]
        half = units // 2
        fh = nf // nh
        out = pl.pallas_call(
            lambda *refs: block_kernel(nf, nh, ng, ny, nx, *refs),
            out_shape=jax.ShapeDtypeStruct((ng, fh, rg, cols_d), BF16),
            in_specs=[vmem, vmem, vmem, any_, any_, any_, any_],
            out_specs=vmem,
            scratch_shapes=[
                pltpu.VMEM(w_out.shape, BF16),
                pltpu.VMEM(w_gate.shape, BF16),
                pltpu.VMEM(w_up.shape, BF16),
                pltpu.VMEM(w_down.shape, BF16),
                pltpu.VMEM((ng, nf, rg, width), BF16),
                pltpu.VMEM((ng, nf, rg, 256), F32),
                pltpu.VMEM((ng, nf, rg, width), BF16),
                pltpu.VMEM((ng, nh, rows // ng // nh, cols_d), BF16),
                pltpu.VMEM((ng, nh, rows // ng // nh, cols_d), BF16),
                pltpu.VMEM((ng, nh, rows // ng // nh, cols_d), BF16),
                pltpu.VMEM((ng, rows // ng, cols_d), BF16),
                pltpu.VMEM((ng, nf, rg, 128), F32),
                pltpu.VMEM((ng, nf, rg, 128), F32),
                pltpu.VMEM((ng, 2, 2, ny, nx, rg, units), BF16),
                pltpu.VMEM((ng, 2, ny, nx, rg, units), BF16),
                pltpu.VMEM((ng, nx, ny, rg, units), BF16),
                pltpu.VMEM((ng, ny, nx, rg, units), BF16),
                pltpu.VMEM((ng, ny, rg, units), BF16),
                pltpu.VMEM((ng, nx, rg, units), BF16),
                pltpu.VMEM((ng, ny, rg, units), BF16),
                pltpu.VMEM((ng, nx, rg, units), BF16),
                pltpu.VMEM((ng, 2, 2, ny, nx, rg, half), BF16),
                pltpu.VMEM((ng, nf, rg, cols_d), BF16),
                pltpu.VMEM((ng, nh, fh, rg, cols_d), BF16),
                dma((4,)),
                *[dma((ng, n)) for n in (
                    nf, nf, nf, nf, nf, nf, nh, nh, nh, nh, nf, nf,
                    2, 2, nx, nx, ny, ny, nx, nx, ny, ny,
                    ny, ny, nx, nx, nx, nx, ny, ny, 2, 2, nh, nh)],
            ],
            compiler_params=pltpu.CompilerParams(
                collective_id=1, has_side_effects=True, vmem_limit_bytes=58 * MIB),
            name="block",
        )(
            mix.reshape(ng, nf, rg, width), stat.reshape(ng, nf, rg, 256),
            norm_gain.reshape(1, -1), w_out, w_gate, w_up, w_down,
        )
        return out.reshape(rows // nh, cols_d)

    placed = (
        P("frames", "heads"), P("frames", None), P(None, "heads"), P(None, "heads"),
        P(None, "heads"), P("heads", "frames"), P("frames"), P("frames", "heads"),
        P("frames", "heads"), P("heads", "frames"),
    )
    return jax.shard_map(
        on_device, mesh=mesh, in_specs=placed, out_specs=P("heads", "frames"), check_vma=False
    )
```

```python
import math

import jax
import jax.numpy as jnp
from jax import lax
from jax.experimental import pallas as pl
from jax.experimental.pallas import tpu as pltpu
from jax.sharding import PartitionSpec as P

HDIM = 128
norm_eps = 1e-06
F32 = jnp.float32
BF16 = jnp.bfloat16
MIB = 2**20


def rcopy(src, dst, ssem, rsem, axis, peer):
    return pltpu.make_async_remote_copy(
        src_ref=src,
        dst_ref=dst,
        send_sem=ssem,
        recv_sem=rsem,
        device_id={axis: peer},
        device_id_type=pl.DeviceIdType.MESH,
    )


def loop(lo, hi, body):
    def step(i, carry):
        body(i)
        return carry

    lax.fori_loop(lo, hi, step, 0)


def flat(value):
    rows, cols = value.shape[-2], value.shape[-1]
    if rows % 16:
        return value.astype(F32).reshape(-1, cols).astype(value.dtype)
    return value.reshape(-1, cols)


def tile_of(size, want):
    return want if size % want == 0 else size


def attend_kernel(
    nf, nh, ng,
    fr, lat, wq, wk, wv,
    mix_out, stat_out,
    fr_all, q_all, wq_v, wkv, acc,
    w_sem, rs_sem, ls_sem, fr_sem, qs_sem, qr_sem,
):
    me = lax.axis_index("frames")
    hz = lax.axis_index("heads")
    width = wq.shape[1]
    heads = width // HDIM
    tokens = fr.shape[1]

    c_q = pltpu.make_async_copy(wq, wq_v, w_sem.at[0])
    c_k = pltpu.make_async_copy(wk, wkv.at[0], w_sem.at[1])
    c_v = pltpu.make_async_copy(wv, wkv.at[1], w_sem.at[2])
    c_q.start()
    c_k.start()
    c_v.start()

    barrier = pltpu.get_barrier_semaphore()

    def greet(d):
        pl.semaphore_signal(
            barrier, inc=1, device_id={"frames": lax.rem(me + d, nf)},
            device_id_type=pl.DeviceIdType.MESH)

    loop(1, nf, greet)
    has_l = hz > 0
    has_r = hz < nh - 1

    @pl.when(has_l)
    def _():
        pl.semaphore_signal(barrier, inc=1, device_id={"heads": hz - 1},
                            device_id_type=pl.DeviceIdType.MESH)

    @pl.when(has_r)
    def _():
        pl.semaphore_signal(barrier, inc=1, device_id={"heads": hz + 1},
                            device_id_type=pl.DeviceIdType.MESH)

    pl.semaphore_wait(barrier, nf - 1 + has_l.astype(jnp.int32) + has_r.astype(jnp.int32))

    def right(s, src, b):
        return rcopy(src, fr_all.at[b], rs_sem.at[s], fr_sem.at[b], "heads", hz + 1)

    def left(s, src, b):
        return rcopy(src, fr_all.at[b], ls_sem.at[s], fr_sem.at[b], "heads", hz - 1)

    @pl.when(has_r)
    def _():
        right(0, fr, hz).start()

    @pl.when(has_l)
    def _():
        left(0, fr, hz).start()

    c_q.wait()
    fh = nf // nh
    per = fh // ng
    inner = lax.rem(me, fh)
    slot = (inner // per * nh + me // fh) * per + lax.rem(inner, per)
    q_all[slot] = jnp.dot(lat[...], wq_v[...], preferred_element_type=F32).astype(BF16)

    def qcopy(d):
        return rcopy(q_all.at[slot], q_all.at[slot], qs_sem.at[d], qr_sem.at[d],
                     "frames", lax.rem(me + d, nf))

    loop(1, nf, lambda d: qcopy(d).start())
    c_k.wait()
    c_v.wait()

    tt = tile_of(tokens, 256)

    def project(x, b, first):
        def tile(i):
            rows = pl.ds(pl.multiple_of(i * tt, tt), tt)
            xb = x[:, rows]
            for w in range(2):
                term = lax.dot_general(xb, wkv[w, b], (((0,), (0,)), ((), ())),
                                       preferred_element_type=F32)
                if first:
                    acc[w, rows, :] = term
                else:
                    acc[w, rows, :] += term
        loop(0, tokens // tt, tile)

    project(fr, hz, True)

    def hop(s):
        lb, rb = hz - s, hz + s

        @pl.when(lb >= 0)
        def _():
            right(s, fr, lb).wait_recv()

            @pl.when(has_r)
            def _():
                right(s, fr_all.at[lb], lb).start()

        @pl.when(rb < nh)
        def _():
            right(s, fr, rb).wait_recv()

            @pl.when(has_l)
            def _():
                left(s, fr_all.at[rb], rb).start()

        @pl.when(lb >= 0)
        def _():
            project(fr_all.at[lb], lb, False)

        @pl.when(rb < nh)
        def _():
            project(fr_all.at[rb], rb, False)

    loop(1, nh, hop)
    loop(1, nf, lambda d: qcopy(d).wait_recv())

    scale = HDIM ** (-0.5)
    latents = mix_out.shape[0]
    lane = lax.broadcasted_iota(jnp.int32, (latents, 128), 1)
    peaks = jnp.zeros((latents, 128), F32)
    sums = jnp.ones((latents, 128), F32)
    for h in range(heads):
        cols = slice(h * HDIM, (h + 1) * HDIM)
        q = flat(q_all[:, :, cols])
        k = acc[0, :, cols].astype(BF16)
        v = acc[1, :, cols].astype(BF16)
        scores = lax.dot_general(q, k, (((1,), (1,)), ((), ())),
                                 preferred_element_type=F32) * scale
        peak = jnp.max(scores, axis=1, keepdims=True)
        weights = jnp.exp(scores - peak)
        total = jnp.sum(weights, axis=1, keepdims=True)
        mixed = jnp.dot(weights.astype(BF16), v, preferred_element_type=F32)
        mix_out[:, cols] = (mixed / total).astype(BF16)
        peaks = jnp.where(lane == h, peak, peaks)
        sums = jnp.where(lane == h, total, sums)
    stat_out[:, :128] = peaks
    stat_out[:, 128:] = sums

    loop(1, nf, lambda d: qcopy(d).wait_send())

    def drain(s):
        @pl.when((hz - s >= 0) & has_r)
        def _():
            right(s, fr, hz).wait_send()

        @pl.when((hz + s < nh) & has_l)
        def _():
            left(s, fr, hz).wait_send()

    loop(0, nh, drain)


def block_kernel(
    nf, nh, ng, ny, nx,
    mix, stat, gain, w_out, w_gate, w_up, w_down,
    out,
    wo, wg, wu, wd,
    rm, rst, att_all, part, rz, lat_all, nrm, sqp, rsq,
    gu, rc, r2a, r2b, s2a, s2b, r3a, r3b, hid, dp, rd,
    w_sem, mix_s, mix_r, st_s, st_r, at_s, at_r, z_s, z_r, l_s, l_r, sq_s, sq_r,
    c_s, c_r, x2_s, x2_r, y2_s, y2_r, x3_s, x3_r, y3_s, y3_r,
    hy_s, hy_r, hx_s, hx_r, gx_s, gx_r, gy_s, gy_r, hc_s, hc_r, d_s, d_r,
):
    me = lax.axis_index("frames")
    hz = lax.axis_index("heads")
    core = lax.rem(me, 2)
    xi = lax.rem(me // 2, nx)
    yi = me // (2 * nx)
    r, width = mix.shape[2], mix.shape[3]
    heads = width // HDIM
    fh = nf // nh
    cols_d = wo.shape[1]
    units = wg.shape[1]
    half = units // 2
    latents = nf * r

    copies = [
        pltpu.make_async_copy(src, dst, w_sem.at[i])
        for i, (src, dst) in enumerate(
            [(w_out, wo), (w_gate, wg), (w_up, wu), (w_down, wd)])
    ]
    for c in copies:
        c.start()

    barrier = pltpu.get_barrier_semaphore()

    def fpeer(d):
        return lax.rem(me + d, nf)

    def zpeer(d):
        return lax.rem(hz + d, nh)

    def xpeer(d):
        return lax.rem(xi + d, nx)

    def ypeer(d):
        return lax.rem(yi + d, ny)

    def xdev(x):
        return (yi * nx + x) * 2 + core

    def ydev(y):
        return (y * nx + xi) * 2 + core

    def greet_f(d):
        pl.semaphore_signal(barrier, inc=1, device_id={"frames": fpeer(d)},
                            device_id_type=pl.DeviceIdType.MESH)

    def greet_z(d):
        pl.semaphore_signal(barrier, inc=1, device_id={"heads": zpeer(d)},
                            device_id_type=pl.DeviceIdType.MESH)

    loop(1, nf, greet_f)
    loop(1, nh, greet_z)
    pl.semaphore_wait(barrier, nf + nh - 2)

    def phases(
        g,
        mix, stat, out, rm, rst, att_all, part, rz, lat_all, nrm, sqp, rsq, gu, rc, r2a, r2b,
        s2a, s2b, r3a, r3b, hid, dp, rd, mix_s, mix_r, st_s, st_r, at_s, at_r, z_s, z_r, l_s,
        l_r, sq_s, sq_r, c_s, c_r, x2_s, x2_r, y2_s, y2_r, x3_s, x3_r, y3_s, y3_r, hy_s, hy_r,
        hx_s, hx_r, gx_s, gx_r, gy_s, gy_r, hc_s, hc_r, d_s, d_r,
    ):
        def mcopy(d):
            return rcopy(mix.at[fpeer(d)], rm.at[d], mix_s.at[d], mix_r.at[d], "frames", fpeer(d))

        def scopy(d):
            return rcopy(stat.at[fpeer(d)], rst.at[d], st_s.at[d], st_r.at[d], "frames", fpeer(d))

        def send_mix(d):
            scopy(d).start()
            mcopy(d).start()

        loop(1, nf, send_mix)
        rm[0] = mix[me]
        rst[0] = stat[me]
        yield
        loop(1, nf, lambda d: scopy(d).wait_recv())
        peak = rst[0, :, :128]
        for d in range(1, nf):
            peak = jnp.maximum(peak, rst[d, :, :128])
        loop(1, nf, lambda d: mcopy(d).wait_recv())
        num = [jnp.zeros((r, HDIM), F32) for _ in range(heads)]
        den = jnp.zeros((r, 128), F32)
        for d in range(nf):
            share = jnp.exp(rst[d, :, :128] - peak) * rst[d, :, 128:]
            den = den + share
            for h in range(heads):
                num[h] = num[h] + share[:, h:h + 1] * rm[d, :, h * HDIM:(h + 1) * HDIM].astype(F32)
        for h in range(heads):
            att_all[me, :, h * HDIM:(h + 1) * HDIM] = (num[h] / den[:, h:h + 1]).astype(BF16)

        def acopy(d):
            return rcopy(att_all.at[me], att_all.at[me], at_s.at[d], at_r.at[d], "frames", fpeer(d))

        loop(1, nf, lambda d: acopy(d).start())
        yield
        loop(1, nf, lambda d: acopy(d).wait_recv())

        if g == 0:
            copies[0].wait()
        att = flat(att_all[...])
        tile = tile_of(cols_d, 512)
        for t in range(cols_d // tile):
            cs = slice(t * tile, (t + 1) * tile)
            res = jnp.dot(att, wo[:, cs], preferred_element_type=F32)
            part[:, :, cs] = res.reshape(nh, latents // nh, tile).astype(BF16)

        def zcopy(d):
            return rcopy(part.at[zpeer(d)], rz.at[d], z_s.at[d], z_r.at[d], "heads", zpeer(d))

        loop(1, nh, lambda d: zcopy(d).start())
        yield
        loop(1, nh, lambda d: zcopy(d).wait_recv())
        state = part[hz].astype(F32)
        for d in range(1, nh):
            state = state + rz[d].astype(F32)
        lat_all[hz] = state.astype(BF16)

        def lcopy(d):
            return rcopy(lat_all.at[hz], lat_all.at[hz], l_s.at[d], l_r.at[d], "heads", zpeer(d))

        loop(1, nh, lambda d: lcopy(d).start())
        yield
        loop(1, nh, lambda d: lcopy(d).wait_recv())

        full = lat_all[...].astype(F32).reshape(latents, cols_d)
        nrm[...] = (full * gain[...]).astype(BF16)
        squares = jnp.sum(full * full, axis=1, keepdims=True)
        sqp[...] = jnp.broadcast_to(squares, (latents, 128)).reshape(nf, r, 128)

        def qcopy(d):
            return rcopy(sqp.at[fpeer(d)], rsq.at[d], sq_s.at[d], sq_r.at[d], "frames", fpeer(d))

        loop(1, nf, lambda d: qcopy(d).start())

        if g == 0:
            copies[1].wait()
            copies[2].wait()
        gt = tile_of(half, 512)

        def ccopy(t):
            return rcopy(gu.at[t, 1 - core], rc.at[t], c_s.at[t], c_r.at[t],
                         "frames", me + 1 - 2 * core)

        for t in range(2):
            for j in range(2):
                weight = (wg, wu)[j]

                def step(k, t=t, j=j, weight=weight):
                    src = pl.ds(pl.multiple_of(t * half + k * gt, gt), gt)
                    dst = pl.ds(pl.multiple_of(j * half + k * gt, gt), gt)
                    res = jnp.dot(nrm[...], weight[:, src], preferred_element_type=F32)
                    res = res.reshape(ny, nx, 2, r, gt).astype(BF16)
                    for c in range(2):
                        gu[t, c, :, :, :, dst] = res[:, :, c]

                loop(0, half // gt, step)
            ccopy(t).start()
        yield

        def x2copy(d):
            return rcopy(gu.at[0, core, :, xpeer(d)], r2a.at[d], x2_s.at[d], x2_r.at[d],
                         "frames", xdev(xpeer(d)))

        def y2copy(d):
            return rcopy(gu.at[1, core, ypeer(d)], r2b.at[d], y2_s.at[d], y2_r.at[d],
                         "frames", ydev(ypeer(d)))

        def merge(t):
            ccopy(t).wait_recv()
            for y in range(ny):
                for x in range(nx):
                    gu[t, core, y, x] = (
                        gu[t, core, y, x].astype(F32) + rc[t, y, x].astype(F32)).astype(BF16)

        merge(0)
        loop(1, nx, lambda d: x2copy(d).start())
        merge(1)
        loop(1, ny, lambda d: y2copy(d).start())
        yield

        def y3copy(d):
            return rcopy(s2a.at[ypeer(d)], r3a.at[d], y3_s.at[d], y3_r.at[d],
                         "frames", ydev(ypeer(d)))

        def x3copy(d):
            return rcopy(s2b.at[xpeer(d)], r3b.at[d], x3_s.at[d], x3_r.at[d],
                         "frames", xdev(xpeer(d)))

        loop(1, nx, lambda d: x2copy(d).wait_recv())
        for y in range(ny):
            total = gu[0, core, y, xi].astype(F32)
            for d in range(1, nx):
                total = total + r2a[d, y].astype(F32)
            s2a[y] = total.astype(BF16)
        loop(1, ny, lambda d: y3copy(d).start())
        loop(1, ny, lambda d: y2copy(d).wait_recv())
        for x in range(nx):
            total = gu[1, core, yi, x].astype(F32)
            for d in range(1, ny):
                total = total + r2b[d, x].astype(F32)
            s2b[x] = total.astype(BF16)
        loop(1, nx, lambda d: x3copy(d).start())
        yield

        loop(1, nf, lambda d: qcopy(d).wait_recv())
        ssum = sqp[me]
        for d in range(1, nf):
            ssum = ssum + rsq[d]
        scale = lax.rsqrt(ssum[:, :1] / (cols_d * nf) + norm_eps)

        def activate(t, total):
            gate = total[:, :half] * scale
            up = total[:, half:] * scale
            hid[t, core, yi, xi] = (gate / (1.0 + jnp.exp(-gate)) * up).astype(BF16)

        def hycopy(d):
            block = hid.at[0, core, yi, xi]
            return rcopy(block, block, hy_s.at[d], hy_r.at[d], "frames", ydev(ypeer(d)))

        def hxcopy(d):
            block = hid.at[1, core, yi, xi]
            return rcopy(block, block, hx_s.at[d], hx_r.at[d], "frames", xdev(xpeer(d)))

        def gxcopy(d):
            block = hid.at[0, core, :, xi]
            return rcopy(block, block, gx_s.at[d], gx_r.at[d], "frames", xdev(xpeer(d)))

        def gycopy(d):
            block = hid.at[1, core, yi]
            return rcopy(block, block, gy_s.at[d], gy_r.at[d], "frames", ydev(ypeer(d)))

        def hccopy(t):
            block = hid.at[t, core]
            return rcopy(block, block, hc_s.at[t], hc_r.at[t], "frames", me + 1 - 2 * core)

        loop(1, ny, lambda d: y3copy(d).wait_recv())
        total = s2a[yi].astype(F32)
        for d in range(1, ny):
            total = total + r3a[d].astype(F32)
        activate(0, total)
        loop(1, ny, lambda d: hycopy(d).start())
        loop(1, nx, lambda d: x3copy(d).wait_recv())
        total = s2b[xi].astype(F32)
        for d in range(1, nx):
            total = total + r3b[d].astype(F32)
        activate(1, total)
        loop(1, nx, lambda d: hxcopy(d).start())
        yield
        loop(1, ny, lambda d: hycopy(d).wait_recv())
        loop(1, nx, lambda d: gxcopy(d).start())
        loop(1, nx, lambda d: hxcopy(d).wait_recv())
        loop(1, ny, lambda d: gycopy(d).start())
        yield
        loop(1, nx, lambda d: gxcopy(d).wait_recv())
        hccopy(0).start()
        loop(1, ny, lambda d: gycopy(d).wait_recv())
        hccopy(1).start()
        yield
        if g == 0:
            copies[3].wait()
        hccopy(0).wait_recv()
        hccopy(1).wait_recv()

        dt = tile_of(cols_d, 256)

        def down(k):
            cs = pl.ds(pl.multiple_of(k * dt, dt), dt)
            res = jnp.dot(flat(hid[0]), wd[:half, cs], preferred_element_type=F32)
            res = res + jnp.dot(flat(hid[1]), wd[half:, cs], preferred_element_type=F32)
            res = res.reshape(2, nf // 2, r, dt).astype(BF16)
            for b in range(nf):
                dp[b, :, cs] = res[b % 2, b // 2]

        loop(0, cols_d // dt, down)

        def dcopy(d):
            return rcopy(dp.at[pl.ds(zpeer(d) * fh, fh)], rd.at[d], d_s.at[d], d_r.at[d],
                         "heads", zpeer(d))

        loop(1, nh, lambda d: dcopy(d).start())
        yield
        loop(1, nh, lambda d: dcopy(d).wait_recv())
        total = lat_all[hz].astype(F32).reshape(fh, r, cols_d) + dp[pl.ds(hz * fh, fh)].astype(F32)
        for d in range(1, nh):
            total = total + rd[d].astype(F32)
        out[...] = total.astype(BF16)

        def drain_f(d):
            scopy(d).wait_send()
            mcopy(d).wait_send()
            acopy(d).wait_send()
            qcopy(d).wait_send()

        def drain_z(d):
            zcopy(d).wait_send()
            lcopy(d).wait_send()
            dcopy(d).wait_send()

        def drain_x(d):
            x2copy(d).wait_send()
            x3copy(d).wait_send()
            hxcopy(d).wait_send()
            gxcopy(d).wait_send()

        def drain_y(d):
            y2copy(d).wait_send()
            y3copy(d).wait_send()
            hycopy(d).wait_send()
            gycopy(d).wait_send()

        loop(1, nf, drain_f)
        loop(1, nh, drain_z)
        loop(1, nx, drain_x)
        loop(1, ny, drain_y)
        for t in range(2):
            ccopy(t).wait_send()
            hccopy(t).wait_send()

    views = [
        mix, stat, out, rm, rst, att_all, part, rz, lat_all, nrm, sqp, rsq, gu, rc, r2a, r2b,
        s2a, s2b, r3a, r3b, hid, dp, rd, mix_s, mix_r, st_s, st_r, at_s, at_r, z_s, z_r, l_s,
        l_r, sq_s, sq_r, c_s, c_r, x2_s, x2_r, y2_s, y2_r, x3_s, x3_r, y3_s, y3_r, hy_s, hy_r,
        hx_s, hx_r, gx_s, gx_r, gy_s, gy_r, hc_s, hc_r, d_s, d_r,
    ]
    running = [phases(g, *[v.at[g] for v in views]) for g in range(ng)]
    while running:
        running = [p for p in running if next(p, running) is None]


def solution(mesh):
    nf, nh = mesh.shape["frames"], mesh.shape["heads"]
    chips = nf // 2
    nx = max(k for k in range(1, math.isqrt(chips) + 1) if chips % k == 0)
    ny = chips // nx
    vmem = pl.BlockSpec(memory_space=pltpu.VMEM)
    any_ = pl.BlockSpec(memory_space=pl.ANY)
    dma = pltpu.SemaphoreType.DMA

    def on_device(frames, latents, w_query, w_key, w_value, w_out, norm_gain, w_gate, w_up, w_down):
        tokens, feats = frames.shape
        r = latents.shape[0]
        width = w_key.shape[1]
        rows = r * nf
        ng = 2 if (nf // nh) % 2 == 0 and r % 32 == 0 else 1
        rg = r // ng
        mix, stat = pl.pallas_call(
            lambda *refs: attend_kernel(nf, nh, ng, *refs),
            out_shape=[
                jax.ShapeDtypeStruct((rows, width), BF16),
                jax.ShapeDtypeStruct((rows, 256), F32),
            ],
            in_specs=[vmem, vmem, any_, any_, any_],
            out_specs=[vmem, vmem],
            scratch_shapes=[
                pltpu.VMEM((nh, feats, tokens), BF16),
                pltpu.VMEM((nf, r, width), BF16),
                pltpu.VMEM(w_query.shape, BF16),
                pltpu.VMEM((2, nh, feats, width), BF16),
                pltpu.VMEM((2, tokens, width), F32),
                dma((3,)), dma((nh,)), dma((nh,)), dma((nh,)), dma((nf,)), dma((nf,)),
            ],
            compiler_params=pltpu.CompilerParams(
                collective_id=0, has_side_effects=True, vmem_limit_bytes=60 * MIB),
            name="attend",
        )(
            frames.T, latents, w_query,
            w_key.reshape(nh, feats, width), w_value.reshape(nh, feats, width),
        )
        cols_d = w_out.shape[1]
        units = w_gate.shape[1]
        half = units // 2
        fh = nf // nh
        out = pl.pallas_call(
            lambda *refs: block_kernel(nf, nh, ng, ny, nx, *refs),
            out_shape=jax.ShapeDtypeStruct((ng, fh, rg, cols_d), BF16),
            in_specs=[vmem, vmem, vmem, any_, any_, any_, any_],
            out_specs=vmem,
            scratch_shapes=[
                pltpu.VMEM(w_out.shape, BF16),
                pltpu.VMEM(w_gate.shape, BF16),
                pltpu.VMEM(w_up.shape, BF16),
                pltpu.VMEM(w_down.shape, BF16),
                pltpu.VMEM((ng, nf, rg, width), BF16),
                pltpu.VMEM((ng, nf, rg, 256), F32),
                pltpu.VMEM((ng, nf, rg, width), BF16),
                pltpu.VMEM((ng, nh, rows // ng // nh, cols_d), BF16),
                pltpu.VMEM((ng, nh, rows // ng // nh, cols_d), BF16),
                pltpu.VMEM((ng, nh, rows // ng // nh, cols_d), BF16),
                pltpu.VMEM((ng, rows // ng, cols_d), BF16),
                pltpu.VMEM((ng, nf, rg, 128), F32),
                pltpu.VMEM((ng, nf, rg, 128), F32),
                pltpu.VMEM((ng, 2, 2, ny, nx, rg, units), BF16),
                pltpu.VMEM((ng, 2, ny, nx, rg, units), BF16),
                pltpu.VMEM((ng, nx, ny, rg, units), BF16),
                pltpu.VMEM((ng, ny, nx, rg, units), BF16),
                pltpu.VMEM((ng, ny, rg, units), BF16),
                pltpu.VMEM((ng, nx, rg, units), BF16),
                pltpu.VMEM((ng, ny, rg, units), BF16),
                pltpu.VMEM((ng, nx, rg, units), BF16),
                pltpu.VMEM((ng, 2, 2, ny, nx, rg, half), BF16),
                pltpu.VMEM((ng, nf, rg, cols_d), BF16),
                pltpu.VMEM((ng, nh, fh, rg, cols_d), BF16),
                dma((4,)),
                *[dma((ng, n)) for n in (
                    nf, nf, nf, nf, nf, nf, nh, nh, nh, nh, nf, nf,
                    2, 2, nx, nx, ny, ny, nx, nx, ny, ny,
                    ny, ny, nx, nx, nx, nx, ny, ny, 2, 2, nh, nh)],
            ],
            compiler_params=pltpu.CompilerParams(
                collective_id=1, has_side_effects=True, vmem_limit_bytes=58 * MIB),
            name="block",
        )(
            mix.reshape(ng, nf, rg, width), stat.reshape(ng, nf, rg, 256),
            norm_gain.reshape(1, -1), w_out, w_gate, w_up, w_down,
        )
        return out.reshape(rows // nh, cols_d)

    placed = (
        P("frames", "heads"), P("frames", None), P(None, "heads"), P(None, "heads"),
        P(None, "heads"), P("heads", "frames"), P("frames"), P("frames", "heads"),
        P("frames", "heads"), P("heads", "frames"),
    )
    return jax.shard_map(
        on_device, mesh=mesh, in_specs=placed, out_specs=P("heads", "frames"), check_vma=False
    )
```
